256 devices in a mesh: dp: 128 (over z, y, x), tensor: 2 (over core).
Axes of the slice: x: 4, y: 4, z: 8, core: 2. Of those that a mesh axis runs over, the one named last changes fastest.
Arguments:
- master: float32 [8, 1536, 5120], P(None, ('dp', 'tensor')), may hold values from -6 to 6
- moment_one: float32 [8, 1536, 5120], P(None, ('dp', 'tensor')), may hold values from -2 to 2
- moment_two: float32 [8, 1536, 5120], P(None, ('dp', 'tensor')), may hold values from 0.01 to 1
- grad: float32 [8, 5120, 1536], P(None, 'dp', 'tensor'), may hold values from -70 to 70
Outputs:
- new_master: float32 [8, 5120, 1536], P(None, 'dp', 'tensor')
- new_moment_one: float32 [8, 5120, 1536], P(None, 'dp', 'tensor')
- new_moment_two: float32 [8, 5120, 1536], P(None, 'dp', 'tensor')
The draws below stay inside these ranges and needn't reach their ends.
All inputs are finite; a program needn't handle non-finite values.
Results may differ from the reference program's by a relative error of at most 0.0003.
Values sent between devices are 32-bit elements; how exact they have to be, the bound alone decides.
A program may use at most 64 MiB of HBM per device.

```python
import math
import jax
import jax.numpy as jnp

D = 5120
MOE_FF = 1536
MATS = 8


def draw_grad(key, part):
    key = jax.random.fold_in(key, 7)
    noise_key, row_key, col_key = jax.random.split(key, 3)
    half = 0.5 * math.log(10.0)
    row_part = jnp.exp(jax.random.uniform(row_key, (MATS, D, 1), jnp.float32, 0.0, half))
    col_part = jnp.exp(jax.random.uniform(col_key, (MATS, 1, MOE_FF), jnp.float32, 0.0, half))
    place = jnp.arange(D, dtype=jnp.float32).reshape(1, D, 1) / D
    noise = jnp.clip(jax.random.normal(noise_key, (MATS, D, MOE_FF), jnp.float32), -4.0, 4.0)
    ramp = jnp.sqrt(1.0 + 2.0 * place)
    return noise * row_part * col_part * ramp


def level_of(stream_key, dims, pieces, smallest, top_value):
    gain = 1.0
    for axis_at, shards_of in pieces:
        heights = jax.random.uniform(jax.random.fold_in(jax.random.fold_in(stream_key, 6), axis_at), (shards_of,), jnp.float32, smallest / len(pieces), top_value / len(pieces))
        gain = gain * jnp.repeat(jnp.exp(heights), dims[axis_at] // shards_of).reshape((-1,) + (1,) * (len(dims) - 1 - axis_at))
    return gain


def normal_values(own_key, dims, scale, reach, pieces=(), held_as=jnp.bfloat16):
    gain = level_of(own_key, dims, pieces, -0.22, 0.18) if pieces else 1.0
    values = jax.random.normal(own_key, dims, jnp.float32) * scale * gain
    return jnp.minimum(jnp.maximum(values, -reach), reach).astype(held_as)


def setup_inputs(seed: int = 0) -> dict:
    arg_keys = jax.random.split(jax.random.key(seed), 5)
    master = normal_values(arg_keys[0], (MATS, MOE_FF, D), 1.0, 6.0, ((1, 256),), jnp.float32)
    moment_one = normal_values(arg_keys[1], (MATS, MOE_FF, D), 0.3, 2.0, ((1, 256),), jnp.float32)
    moment_two = jnp.clip(jnp.exp(math.log(1.0) - 4.6051702 * jax.random.uniform(arg_keys[2], (MATS, MOE_FF, D), jnp.float32) ** level_of(arg_keys[2], (MATS, MOE_FF, D), ((1, 256),), -0.2, 0.2)), 0.01, 1.0)
    grad = draw_grad(jax.random.fold_in(arg_keys[4], 71), 0)
    return dict(master=master, moment_one=moment_one, moment_two=moment_two, grad=grad)


bias_first = 0.9999734386011124
bias_second = 0.994079470779666

def reference(master, moment_one, moment_two, grad):
    weights = jnp.transpose(master, (0, 2, 1))
    first = jnp.transpose(moment_one, (0, 2, 1))
    second = jnp.transpose(moment_two, (0, 2, 1))
    total = jnp.sum(grad * grad)
    count = float(MATS * D * MOE_FF)
    scale = jnp.minimum(jnp.float32(1.0), 0.5 * jnp.sqrt(jnp.float32(count)) / (jnp.sqrt(total) + 1e-06))
    clipped = scale * grad
    new_first = 0.9 * first + 0.1 * clipped
    new_second = 0.95 * second + 0.05 * clipped * clipped
    update = new_first / bias_first / (jnp.sqrt(new_second / bias_second) + 1e-08)
    new_weights = weights * (1.0 - 0.05 * 0.1) - 0.05 * update
    return (new_weights, new_first, new_second)
```

```python
import jax
import jax.numpy as jnp
from jax import lax
from jax.experimental import pallas as pl
from jax.experimental.pallas import tpu as pltpu
from jax.sharding import PartitionSpec as P

D = 5120
MOE_FF = 1536
MATS = 8
ROWS = 6
BLOCK = 40
MESH = pl.DeviceIdType.MESH

bias_first = 0.9999734386011124
bias_second = 0.994079470779666
COUNT = float(MATS * D * MOE_FF)


def pack_group(xin, src, zt, part):
    lane = lax.broadcasted_iota(jnp.int32, (8, 128), 1)
    base = pl.multiple_of(zt * 640, 128)
    for h in range(ROWS):
        tiles = []
        for a in range(3):
            row = []
            for t in range(5):
                v = xin[a, h, :, pl.ds(base + 128 * t, 128)]
                row.append(v if a == 0 else pltpu.roll(v, 40 * a, 1))
            tiles.append(row)
        for p in range(16):
            start = (40 * p) % 128
            t0 = (40 * p) // 128
            u = (lane + (128 - start)) & 127
            pieces = []
            for a in range(3):
                piece = tiles[a][t0]
                if start + 40 > 128:
                    piece = jnp.where(u < 40 * a + 128 - start, piece, tiles[a][t0 + 1])
                pieces.append(piece)
            out = jnp.where(u < 40, pieces[0], jnp.where(u < 80, pieces[1], pieces[2]))
            if h == 0:
                out = jnp.where(u < 120, out, part)
            src[zt * 16 + p, 8 * h : 8 * h + 8, :] = out


def kernel(
    x0, x1, x2, g_hbm, o0, o1, o2,
    xin, gv, src, arr, wide, outv, sumv, sib,
    in_sem, g_sem, send_sem, recv_sem, sib_send, sib_recv, out_sem,
):
    s = lax.axis_index("dp")
    c = lax.axis_index("tensor")
    z = s // 16
    plane = s % 16
    half = z // 4
    dl = 2 * (s % 64) + c
    group = (z % 4) // 2
    mine = half == c

    gcopy = pltpu.make_async_copy(g_hbm, gv, g_sem)
    gcopy.start()

    def in_copies(zt):
        cols = pl.ds(pl.multiple_of(zt * 640, 128), 640)
        return [
            pltpu.make_async_copy(x.at[:, :, cols], xin.at[a, :, :, cols], in_sem.at[zt])
            for a, x in enumerate((x0, x1, x2))
        ]

    def order(i):
        return 2 * (1 - i % 2) + (1 - i // 2)

    def start_in(j, carry):
        for copy in in_copies(z ^ (2 * order(j // 2) + j % 2)):
            copy.start()
        return carry

    lax.fori_loop(0, 8, start_in, 0)

    barrier = pltpu.get_barrier_semaphore()

    def greet(i, carry):
        peer, core = c * 64 + i // 2, i % 2

        @pl.when(jnp.logical_or(peer != s, core != c))
        def _():
            pl.semaphore_signal(barrier, inc=1, device_id=(peer, core), device_id_type=MESH)

        return carry

    lax.fori_loop(0, 128, greet, 0)

    @pl.when(jnp.logical_not(mine))
    def _():
        pl.semaphore_signal(barrier, inc=1, device_id=(s, 1 - c), device_id_type=MESH)

    gcopy.wait()

    def squares(m, acc):
        for i in range(5):
            for j in range(6):
                v = gv[m, 8 * i : 8 * i + 8, 128 * j : 128 * j + 128]
                acc = acc + v * v
        return acc

    acc = lax.fori_loop(0, MATS, squares, jnp.zeros((8, 128), jnp.float32))
    part = jnp.broadcast_to(jnp.sum(acc, axis=(0, 1), keepdims=True), (8, 128))

    def message(t):
        return pltpu.make_async_remote_copy(
            src_ref=src.at[t],
            dst_ref=arr.at[pl.ds(pl.multiple_of(48 * dl, 8), 48)],
            send_sem=send_sem,
            recv_sem=recv_sem.at[group],
            device_id=(t, half),
            device_id_type=MESH,
        )

    def phase(i, carry):
        a = order(i)

        def pack(e, inner):
            zt = z ^ (2 * a + e)
            for copy in in_copies(zt):
                copy.wait()
            pack_group(xin, src, zt, part)
            return inner

        lax.fori_loop(0, 2, pack, 0)

        @pl.when(i == 0)
        def _():
            pl.semaphore_wait(barrier, 128)

        def send(r, inner):
            t = (z ^ (2 * a + r % 2)) * 16 + (plane ^ (r // 2))
            own = jnp.logical_and(t == s, mine)

            @pl.when(jnp.logical_not(own))
            def _():
                message(t).start()

            @pl.when(own)
            def _():
                pltpu.make_async_copy(
                    src.at[t], arr.at[pl.ds(pl.multiple_of(48 * dl, 8), 48)], recv_sem.at[group]
                ).start()

            return inner

        lax.fori_loop(0, 32, send, 0)
        return carry

    lax.fori_loop(0, 4, phase, 0)

    def gather(i, carry):
        first = (z // 2) ^ jnp.where(mine, 1, 3)
        grp = jnp.where(i == 0, first, first ^ 1) % 2
        rows = pl.ds(pl.multiple_of(grp * 3072, 8), 3072)
        pltpu.make_async_copy(arr.at[rows], arr.at[rows], recv_sem.at[grp]).wait()

        def flip(m, inner):
            for t in range(3):
                tile = grp * 3 + t
                x = arr[pl.ds(tile * 1024 + m, 128, 8), :]
                wide[tile, m] = x.T
            return inner

        lax.fori_loop(0, MATS, flip, 0)
        return carry

    lax.fori_loop(0, 2, gather, 0)

    def partial(d, acc):
        return acc + arr[pl.ds(pl.multiple_of(d * 48, 8), 8), :]

    halves = lax.fori_loop(0, 128, partial, jnp.zeros((8, 128), jnp.float32))
    lane = lax.broadcasted_iota(jnp.int32, (8, 128), 1)
    sub = lax.broadcasted_iota(jnp.int32, (8, 128), 0)
    begin = (40 * plane) % 128
    spot = jnp.logical_and((lane + (128 - begin)) % 128 == 120, sub == 0)
    half_sum = jnp.sum(jnp.where(spot, halves, 0.0), axis=(0, 1), keepdims=True)
    sumv[...] = jnp.broadcast_to(half_sum, (8, 128))
    swap = pltpu.make_async_remote_copy(
        src_ref=sumv,
        dst_ref=sib,
        send_sem=sib_send,
        recv_sem=sib_recv,
        device_id=(s, 1 - c),
        device_id_type=MESH,
    )
    swap.start()
    swap.wait()
    total = (sumv[...] + sib[...])[0:1, 0:1]
    scale = jnp.minimum(1.0, 0.5 * jnp.sqrt(jnp.float32(COUNT)) / (jnp.sqrt(total) + 1e-06))
    scale = jnp.broadcast_to(scale, (8, 128))

    def out_copies(m):
        return [
            pltpu.make_async_copy(outv.at[a, m], o.at[m], out_sem) for a, o in enumerate((o0, o1, o2))
        ]

    def update(m, carry):
        for w in range(5):
            spots = [pl.multiple_of(8 * ((5 * plane + 5 * a + w) % 16), 8) for a in range(3)]
            for t in range(6):
                rows = slice(8 * w, 8 * w + 8)
                cols = slice(128 * t, 128 * t + 128)
                weights = wide[t, m, pl.ds(spots[0], 8), :]
                first = wide[t, m, pl.ds(spots[1], 8), :]
                second = wide[t, m, pl.ds(spots[2], 8), :]
                clipped = scale * gv[m, rows, cols]
                new_first = 0.9 * first + 0.1 * clipped
                new_second = 0.95 * second + 0.05 * clipped * clipped
                step = new_first / bias_first / (jnp.sqrt(new_second / bias_second) + 1e-08)
                outv[0, m, rows, cols] = weights * (1.0 - 0.05 * 0.1) - 0.05 * step
                outv[1, m, rows, cols] = new_first
                outv[2, m, rows, cols] = new_second
        for copy in out_copies(m):
            copy.start()
        return carry

    lax.fori_loop(0, MATS, update, 0)
    for a, o in enumerate((o0, o1, o2)):
        pltpu.make_async_copy(outv.at[a], o, out_sem).wait()
    pltpu.make_async_copy(src.at[pl.ds(0, 127)], src.at[pl.ds(0, 127)], send_sem).wait()

    @pl.when(jnp.logical_not(mine))
    def _():
        pltpu.make_async_copy(src.at[127], src.at[127], send_sem).wait()


def local(master, moment_one, moment_two, grad):
    shape = jax.ShapeDtypeStruct(grad.shape, jnp.float32)
    hbm = pl.BlockSpec(memory_space=pl.ANY)
    stored = [jnp.transpose(x, (1, 0, 2)) for x in (master, moment_one, moment_two)]
    return pl.pallas_call(
        kernel,
        name="regroup_adamw",
        out_shape=(shape, shape, shape),
        in_specs=[hbm] * 4,
        out_specs=(hbm, hbm, hbm),
        scratch_shapes=[
            pltpu.VMEM((3, ROWS, MATS, D), jnp.float32),
            pltpu.VMEM((MATS, BLOCK, 768), jnp.float32),
            pltpu.VMEM((128, 48, 128), jnp.float32),
            pltpu.VMEM((128 * 48, 128), jnp.float32),
            pltpu.VMEM((6, MATS, 128, 128), jnp.float32),
            pltpu.VMEM((3, MATS, BLOCK, 768), jnp.float32),
            pltpu.VMEM((8, 128), jnp.float32),
            pltpu.VMEM((8, 128), jnp.float32),
            pltpu.SemaphoreType.DMA((8,)),
            pltpu.SemaphoreType.DMA,
            pltpu.SemaphoreType.DMA,
            pltpu.SemaphoreType.DMA((2,)),
            pltpu.SemaphoreType.DMA,
            pltpu.SemaphoreType.DMA,
            pltpu.SemaphoreType.DMA,
        ],
        compiler_params=pltpu.CompilerParams(
            collective_id=0, has_side_effects=True, vmem_limit_bytes=40 * 2**20
        ),
        cost_estimate=pl.CostEstimate(
            flops=8_000_000, bytes_accessed=7_000_000, transcendentals=500_000
        ),
    )(*stored, grad)


def solution(mesh):
    placed = (
        P(None, ("dp", "tensor"), None),
        P(None, ("dp", "tensor"), None),
        P(None, ("dp", "tensor"), None),
        P(None, "dp", "tensor"),
    )
    return jax.shard_map(
        local,
        mesh=mesh,
        in_specs=placed,
        out_specs=(P(None, "dp", "tensor"), P(None, "dp", "tensor"), P(None, "dp", "tensor")),
        check_vma=False,
    )
```

```python
import jax
import jax.numpy as jnp
from jax import lax
from jax.experimental import pallas as pl
from jax.experimental.pallas import tpu as pltpu
from jax.sharding import PartitionSpec as P

D = 5120
MOE_FF = 1536
MATS = 8
ROWS = 6
BLOCK = 40
MESH = pl.DeviceIdType.MESH

bias_first = 0.9999734386011124
bias_second = 0.994079470779666
COUNT = float(MATS * D * MOE_FF)


def pack_group(xin, src, zt):
    lane = lax.broadcasted_iota(jnp.int32, (8, 128), 1)
    base = pl.multiple_of(zt * 640, 128)
    for h in range(ROWS):
        tiles = []
        for a in range(3):
            row = []
            for t in range(5):
                v = xin[a, h, :, pl.ds(base + 128 * t, 128)]
                row.append(v if a == 0 else pltpu.roll(v, 40 * a, 1))
            tiles.append(row)
        for p in range(16):
            start = (40 * p) % 128
            t0 = (40 * p) // 128
            u = (lane + (128 - start)) & 127
            pieces = []
            for a in range(3):
                piece = tiles[a][t0]
                if start + 40 > 128:
                    piece = jnp.where(u < 40 * a + 128 - start, piece, tiles[a][t0 + 1])
                pieces.append(piece)
            out = jnp.where(u < 40, pieces[0], jnp.where(u < 80, pieces[1], pieces[2]))
            src[zt * 16 + p, 8 * h : 8 * h + 8, :] = out


def regroup(
    x0, x1, x2, g_hbm, wide, gv, total,
    xin, src, arr, mine_sum, plane_sums, col_sums, sib_sum,
    in_sem, g_sem, send_sem, recv_sem, small_send, plane_recv, col_recv, sib_recv, col_sem,
):
    s = lax.axis_index("dp")
    c = lax.axis_index("tensor")
    z = s // 16
    plane = s % 16
    half = z // 4
    dl = 2 * (s % 64) + c
    mine = half == c

    barrier = pltpu.get_barrier_semaphore()
    for i in range(1, 16):
        for core in range(2):
            pl.semaphore_signal(barrier, inc=1, device_id=(s ^ i, core), device_id_type=MESH)
    for i in range(1, 8):
        pl.semaphore_signal(barrier, inc=1, device_id=(s ^ (16 * i), c), device_id_type=MESH)
    pl.semaphore_signal(barrier, inc=1, device_id=(s, 1 - c), device_id_type=MESH)

    def in_copies(zt):
        cols = pl.ds(pl.multiple_of(zt * 640, 128), 640)
        return [
            pltpu.make_async_copy(x.at[:, :, cols], xin.at[a, :, :, cols], in_sem.at[zt])
            for a, x in enumerate((x0, x1, x2))
        ]

    for zt in range(8):
        for copy in in_copies(zt):
            copy.start()
    gcopy = pltpu.make_async_copy(g_hbm, gv, g_sem)
    gcopy.start()

    def pack(zt, carry):
        for copy in in_copies(zt):
            copy.wait()
        pack_group(xin, src, zt)
        return carry

    lax.fori_loop(0, 4, pack, 0)
    pl.semaphore_wait(barrier, 38)
    for i in range(1, 8):
        pl.semaphore_signal(col_sem, inc=1, device_id=(s ^ (16 * i), c), device_id_type=MESH)
    lax.fori_loop(4, 8, pack, 0)
    pl.semaphore_wait(col_sem, 7)

    slot = arr.at[pl.ds(pl.multiple_of(48 * dl, 8), 48)]

    def send(j, carry):
        for e in range(8):
            t = s ^ (16 * (7 - e)) ^ (j ^ (2 * e))
            message = pltpu.make_async_remote_copy(
                src_ref=src.at[t],
                dst_ref=slot,
                send_sem=send_sem,
                recv_sem=recv_sem,
                device_id=(t, half),
                device_id_type=MESH,
            )
            if e < 7:
                message.start()
            else:
                own = jnp.logical_and(j == 14, mine)
                pl.when(jnp.logical_not(own))(message.start)
                pl.when(own)(pltpu.make_async_copy(src.at[t], slot, recv_sem).start)
        return carry

    def small(dst, recv, peer, core):
        return pltpu.make_async_remote_copy(
            src_ref=mine_sum,
            dst_ref=dst,
            send_sem=small_send,
            recv_sem=recv,
            device_id=(peer, core),
            device_id_type=MESH,
        )

    lax.fori_loop(0, 2, send, 0)

    gcopy.wait()

    def squares(m, acc):
        for i in range(5):
            for j in range(6):
                v = gv[m, 8 * i : 8 * i + 8, 128 * j : 128 * j + 128]
                acc = acc + v * v
        return acc

    acc = lax.fori_loop(0, MATS, squares, jnp.zeros((8, 128), jnp.float32))
    part = jnp.broadcast_to(jnp.sum(acc, axis=(0, 1), keepdims=True), (1, 128))
    mine_sum[0] = part
    plane_sums[plane] = part
    plane_out = [small(plane_sums.at[pl.ds(plane, 1)], plane_recv, s ^ i, c) for i in range(1, 16)]
    for copy in plane_out:
        copy.start()
    lax.fori_loop(2, 8, send, 0)
    for copy in plane_out:
        copy.wait_send()
    first15 = plane_sums.at[pl.ds(0, 15)]
    pltpu.make_async_copy(first15, first15, plane_recv).wait()
    part = jnp.sum(plane_sums[...], axis=0)
    mine_sum[0] = part
    col_sums[z] = part
    col_out = [small(col_sums.at[pl.ds(z, 1)], col_recv, s ^ (16 * i), c) for i in range(1, 8)]
    for copy in col_out:
        copy.start()
    lax.fori_loop(8, 16, send, 0)
    for copy in col_out:
        copy.wait_send()
    first7 = col_sums.at[pl.ds(0, 7)]
    pltpu.make_async_copy(first7, first7, col_recv).wait()
    part = jnp.sum(col_sums[...], axis=0)
    mine_sum[0] = part
    swap = small(sib_sum, sib_recv, s, 1 - c)
    swap.start()
    swap.wait()
    total[...] = part + sib_sum[0]

    pltpu.make_async_copy(arr, arr, recv_sem).wait()

    def flip(m, carry):
        for t in range(6):
            wide[t, m] = arr[pl.ds(t * 1024 + m, 128, 8), :].T
        return carry

    lax.fori_loop(0, MATS, flip, 0)

    sent = src.at[pl.ds(0, 127)]
    pltpu.make_async_copy(sent, sent, send_sem).wait()

    @pl.when(jnp.logical_not(mine))
    def _():
        pltpu.make_async_copy(src.at[127], src.at[127], send_sem).wait()


def adamw(wide, gv, total, o0, o1, o2, outv, out_sem):
    plane = lax.axis_index("dp") % 16
    limit = 0.5 * jnp.sqrt(jnp.float32(COUNT))
    scale = jnp.minimum(1.0, limit / (jnp.sqrt(total[...]) + 1e-06))
    scale = jnp.broadcast_to(scale, (8, 128))

    def update(m, carry):
        for w in range(5):
            spots = [pl.multiple_of(8 * ((5 * plane + 5 * a + w) % 16), 8) for a in range(3)]
            for t in range(6):
                rows = slice(8 * w, 8 * w + 8)
                cols = slice(128 * t, 128 * t + 128)
                weights = wide[t, m, pl.ds(spots[0], 8), :]
                first = wide[t, m, pl.ds(spots[1], 8), :]
                second = wide[t, m, pl.ds(spots[2], 8), :]
                clipped = scale * gv[m, rows, cols]
                new_first = 0.9 * first + 0.1 * clipped
                new_second = 0.95 * second + 0.05 * clipped * clipped
                step = new_first / bias_first / (jnp.sqrt(new_second / bias_second) + 1e-08)
                outv[0, m, rows, cols] = weights * (1.0 - 0.05 * 0.1) - 0.05 * step
                outv[1, m, rows, cols] = new_first
                outv[2, m, rows, cols] = new_second
        for a, o in enumerate((o0, o1, o2)):
            pltpu.make_async_copy(outv.at[a, m], o.at[m], out_sem).start()
        return carry

    lax.fori_loop(0, MATS, update, 0)
    for a, o in enumerate((o0, o1, o2)):
        pltpu.make_async_copy(outv.at[a], o, out_sem).wait()


def local(master, moment_one, moment_two, grad):
    shape = jax.ShapeDtypeStruct(grad.shape, jnp.float32)
    hbm = pl.BlockSpec(memory_space=pltpu.HBM)
    vmem = pl.BlockSpec(memory_space=pltpu.VMEM)
    stored = [
        pltpu.with_memory_space_constraint(jnp.transpose(x, (1, 0, 2)), pltpu.HBM)
        for x in (master, moment_one, moment_two)
    ]
    grad = pltpu.with_memory_space_constraint(grad, pltpu.HBM)
    wide, gv, total = pl.pallas_call(
        regroup,
        name="regroup",
        out_shape=(
            pltpu.VMEM((6, MATS, 128, 128), jnp.float32),
            pltpu.VMEM(grad.shape, jnp.float32),
            pltpu.VMEM((1, 128), jnp.float32),
        ),
        in_specs=[hbm] * 4,
        out_specs=(vmem, vmem, vmem),
        scratch_shapes=[
            pltpu.VMEM((3, ROWS, MATS, D), jnp.float32),
            pltpu.VMEM((128, 48, 128), jnp.float32),
            pltpu.VMEM((128 * 48, 128), jnp.float32),
            pltpu.VMEM((1, 1, 128), jnp.float32),
            pltpu.VMEM((16, 1, 128), jnp.float32),
            pltpu.VMEM((8, 1, 128), jnp.float32),
            pltpu.VMEM((1, 1, 128), jnp.float32),
            pltpu.SemaphoreType.DMA((8,)),
            pltpu.SemaphoreType.DMA,
            pltpu.SemaphoreType.DMA,
            pltpu.SemaphoreType.DMA,
            pltpu.SemaphoreType.DMA,
            pltpu.SemaphoreType.DMA,
            pltpu.SemaphoreType.DMA,
            pltpu.SemaphoreType.DMA,
            pltpu.SemaphoreType.REGULAR,
        ],
        compiler_params=pltpu.CompilerParams(
            collective_id=0, has_side_effects=True, vmem_limit_bytes=24 * 2**20
        ),
    )(*stored, grad)
    return pl.pallas_call(
        adamw,
        name="adamw",
        out_shape=(shape, shape, shape),
        in_specs=[vmem] * 3,
        out_specs=(hbm, hbm, hbm),
        scratch_shapes=[
            pltpu.VMEM((3, MATS, BLOCK, 768), jnp.float32),
            pltpu.SemaphoreType.DMA,
        ],
        compiler_params=pltpu.CompilerParams(vmem_limit_bytes=24 * 2**20),
    )(wide, gv, total)


def solution(mesh):
    placed = (
        P(None, ("dp", "tensor"), None),
        P(None, ("dp", "tensor"), None),
        P(None, ("dp", "tensor"), None),
        P(None, "dp", "tensor"),
    )
    return jax.shard_map(
        local,
        mesh=mesh,
        in_specs=placed,
        out_specs=(P(None, "dp", "tensor"), P(None, "dp", "tensor"), P(None, "dp", "tensor")),
        check_vma=False,
    )
```

```python
import jax
import jax.numpy as jnp
from jax import lax
from jax.experimental import pallas as pl
from jax.experimental.pallas import tpu as pltpu
from jax.sharding import PartitionSpec as P

D = 5120
MOE_FF = 1536
MATS = 8
ROWS = 6
BLOCK = 40
MESH = pl.DeviceIdType.MESH

bias_first = 0.9999734386011124
bias_second = 0.994079470779666
COUNT = float(MATS * D * MOE_FF)


def pack_group(xin, src, zt):
    lane = lax.broadcasted_iota(jnp.int32, (8, 128), 1)
    row = lax.broadcasted_iota(jnp.int32, (8, 128), 0)
    low = row < 3
    off1 = jnp.where(low, 80, 72)
    off2 = jnp.where(low, 120, jnp.where(row == 3, 104, 88))
    base = pl.multiple_of(zt * 640, 128)

    def load(a, h, t):
        return xin[a, h, :, pl.ds(base + 128 * t, 128)]

    for h in range(ROWS):
        tiles = [
            [load(a, h, t) if a == 0 else pltpu.roll(load(a, h, t), 40 * a, 1) for t in range(5)]
            for a in range(3)
        ]
        if h < 5:
            extra = [pltpu.roll(load(2, 5, t), 120 - 8 * h, 1) for t in range(5)]
        else:
            fill1, fill2 = [], []
            for t in range(5):
                x, y = load(0, 5, t), load(1, 5, t)
                up = [pltpu.roll(pltpu.roll(y, 8 - d, 0), k, 1) for d, k in ((5, 120), (2, 72), (4, 104), (3, 88))]
                fill1.append(jnp.where(low, pltpu.roll(pltpu.roll(x, 3, 0), 80, 1), up[1]))
                fill2.append(jnp.where(low, up[0], jnp.where(row == 3, up[2], up[3])))
        for p in range(16):
            start = (40 * p) % 128
            t0 = (40 * p) // 128
            u = (lane + (128 - start)) & 127
            split = start + 40 > 128

            def pick(v, offset):
                if not split:
                    return v[t0]
                return jnp.where(u - offset < 128 - start, v[t0], v[t0 + 1])

            first, second = pick(tiles[0], 0), pick(tiles[1], 40)
            if h < 5:
                third = pick(tiles[2], 80)
                out = jnp.where(u < 40, first, jnp.where(u < 80, second, third))
                src[zt * 16 + p, 8 * h : 8 * h + 8, :] = jnp.where(
                    u < 120, out, extra[(5 * p + h) // 16]
                )
            else:
                last = jnp.logical_or(u >= 120, jnp.logical_and(u >= 112, row >= 3))
                third = jnp.where(last, pick(fill2, off2), pick(fill1, off1))
                out = jnp.where(u < 40, first, jnp.where(u < 80, second, third))
                src[zt * 16 + p, 40:45, :] = out[0:5]


def regroup(
    x0, x1, x2, g_hbm, arr, gv, total,
    xin, src, mine_sum, plane_sums, col_sums, sib_sum,
    in_sem, g_sem, send_sem, recv_sem, small_send, plane_recv, col_recv, sib_recv, col_sem,
):
    s = lax.axis_index("dp")
    c = lax.axis_index("tensor")
    z = s // 16
    plane = s % 16
    half = z // 4
    dl = 2 * (s % 64) + c
    mine = half == c

    barrier = pltpu.get_barrier_semaphore()
    for i in range(1, 16):
        for core in range(2):
            pl.semaphore_signal(barrier, inc=1, device_id=(s ^ i, core), device_id_type=MESH)
    for i in range(1, 8):
        pl.semaphore_signal(barrier, inc=1, device_id=(s ^ (16 * i), c), device_id_type=MESH)
    pl.semaphore_signal(barrier, inc=1, device_id=(s, 1 - c), device_id_type=MESH)

    def in_copies(zt):
        cols = pl.ds(pl.multiple_of(zt * 640, 128), 640)
        return [
            pltpu.make_async_copy(x.at[:, :, cols], xin.at[a, :, :, cols], in_sem.at[zt])
            for a, x in enumerate((x0, x1, x2))
        ]

    for zt in range(8):
        for copy in in_copies(zt):
            copy.start()
    gcopy = pltpu.make_async_copy(g_hbm, gv, g_sem)
    gcopy.start()

    def pack(zt, carry):
        for copy in in_copies(zt):
            copy.wait()
        pack_group(xin, src, zt)
        return carry

    lax.fori_loop(0, 4, pack, 0)
    pl.semaphore_wait(barrier, 38)
    for i in range(1, 8):
        pl.semaphore_signal(col_sem, inc=1, device_id=(s ^ (16 * i), c), device_id_type=MESH)
    lax.fori_loop(4, 8, pack, 0)
    pl.semaphore_wait(col_sem, 7)

    slot = arr.at[pl.ds(pl.multiple_of(48 * dl, 8), 45)]

    def send(j, carry):
        for e in range(8):
            t = s ^ (16 * (7 - e)) ^ (j ^ (2 * e))
            message = pltpu.make_async_remote_copy(
                src_ref=src.at[t],
                dst_ref=slot,
                send_sem=send_sem,
                recv_sem=recv_sem,
                device_id=(t, half),
                device_id_type=MESH,
            )
            if e < 7:
                message.start()
            else:
                own = jnp.logical_and(j == 14, mine)
                pl.when(jnp.logical_not(own))(message.start)
                pl.when(own)(pltpu.make_async_copy(src.at[t], slot, recv_sem).start)
        return carry

    def small(dst, recv, peer, core):
        return pltpu.make_async_remote_copy(
            src_ref=mine_sum,
            dst_ref=dst,
            send_sem=small_send,
            recv_sem=recv,
            device_id=(peer, core),
            device_id_type=MESH,
        )

    lax.fori_loop(0, 2, send, 0)

    gcopy.wait()

    def squares(m, acc):
        for i in range(5):
            for j in range(6):
                v = gv[m, 8 * i : 8 * i + 8, 128 * j : 128 * j + 128]
                acc = acc + v * v
        return acc

    acc = lax.fori_loop(0, MATS, squares, jnp.zeros((8, 128), jnp.float32))
    part = jnp.broadcast_to(jnp.sum(acc, axis=(0, 1), keepdims=True), (1, 128))
    mine_sum[0] = part
    plane_sums[plane] = part
    plane_out = [small(plane_sums.at[pl.ds(plane, 1)], plane_recv, s ^ i, c) for i in range(1, 16)]
    for copy in plane_out:
        copy.start()
    lax.fori_loop(2, 8, send, 0)
    for copy in plane_out:
        copy.wait_send()
    first15 = plane_sums.at[pl.ds(0, 15)]
    pltpu.make_async_copy(first15, first15, plane_recv).wait()
    part = jnp.sum(plane_sums[...], axis=0)
    mine_sum[0] = part
    col_sums[z] = part
    col_out = [small(col_sums.at[pl.ds(z, 1)], col_recv, s ^ (16 * i), c) for i in range(1, 8)]
    for copy in col_out:
        copy.start()
    lax.fori_loop(8, 16, send, 0)
    for copy in col_out:
        copy.wait_send()
    first7 = col_sums.at[pl.ds(0, 7)]
    pltpu.make_async_copy(first7, first7, col_recv).wait()
    part = jnp.sum(col_sums[...], axis=0)
    mine_sum[0] = part
    swap = small(sib_sum, sib_recv, s, 1 - c)
    swap.start()
    swap.wait()
    total[...] = part + sib_sum[0]

    pltpu.make_async_copy(src, src, recv_sem).wait()
    sent = src.at[pl.ds(0, 127)]
    pltpu.make_async_copy(sent, sent, send_sem).wait()

    @pl.when(jnp.logical_not(mine))
    def _():
        pltpu.make_async_copy(src.at[127], src.at[127], send_sem).wait()


def adamw(arr, gv, total, o0, o1, o2, wide, outv, out_sem):
    plane = lax.axis_index("dp") % 16
    limit = 0.5 * jnp.sqrt(jnp.float32(COUNT))
    scale = jnp.minimum(1.0, limit / (jnp.sqrt(total[...]) + 1e-06))
    scale = jnp.broadcast_to(scale, (8, 128))
    lane = lax.broadcasted_iota(jnp.int32, (8, 128), 1)
    sixth = [(lane + 128 * t) % 6 == 5 for t in range(3)]

    def slot(t, m, j):
        return wide[t, m, pl.ds(pl.multiple_of(8 * ((5 * plane + j) % 16), 8), 8), :]

    def update(m, late):
        for t in range(6):
            wide[t, m] = arr[pl.ds(t * 1024 + m, 128, 8), :].T
        spare = [slot(t, m, 15) for t in range(6)]
        for w in range(5):
            moved = [pltpu.roll(v, 5 - w, 1) for v in spare]
            for t in range(6):
                rows = slice(8 * w, 8 * w + 8)
                cols = slice(128 * t, 128 * t + 128)
                weights = slot(t, m, w)
                first = slot(t, m, 5 + w)
                back = moved[t] if t % 3 == 0 else jnp.where(lane < 5 - w, moved[t - 1], moved[t])
                second = jnp.where(sixth[t % 3], back, slot(t, m, 10 + w))
                if late:
                    weights = jnp.where(sixth[t % 3], slot(t, m - 5, 10 + w), weights)
                    if w == 0:
                        other = slot(t, m - 5, 15)
                    elif m < 7:
                        other = slot(t, m - 2, 9 + w)
                    else:
                        other = slot(t, 3 + (w - 1) // 2, 14 + (w - 1) % 2)
                    first = jnp.where(sixth[t % 3], other, first)
                clipped = scale * gv[m, rows, cols]
                new_first = 0.9 * first + 0.1 * clipped
                new_second = 0.95 * second + 0.05 * clipped * clipped
                step = new_first / bias_first / (jnp.sqrt(new_second / bias_second) + 1e-08)
                outv[0, m, rows, cols] = weights * (1.0 - 0.05 * 0.1) - 0.05 * step
                outv[1, m, rows, cols] = new_first
                outv[2, m, rows, cols] = new_second
        for a, o in enumerate((o0, o1, o2)):
            pltpu.make_async_copy(outv.at[a, m], o.at[m], out_sem).start()

    def early(m, carry):
        update(m, False)
        return carry

    lax.fori_loop(0, 5, early, 0)
    for m in range(5, MATS):
        update(m, True)
    for a, o in enumerate((o0, o1, o2)):
        pltpu.make_async_copy(outv.at[a], o, out_sem).wait()


def local(master, moment_one, moment_two, grad):
    shape = jax.ShapeDtypeStruct(grad.shape, jnp.float32)
    hbm = pl.BlockSpec(memory_space=pltpu.HBM)
    vmem = pl.BlockSpec(memory_space=pltpu.VMEM)
    stored = [
        pltpu.with_memory_space_constraint(jnp.transpose(x, (1, 0, 2)), pltpu.HBM)
        for x in (master, moment_one, moment_two)
    ]
    grad = pltpu.with_memory_space_constraint(grad, pltpu.HBM)
    arrived, gv, total = pl.pallas_call(
        regroup,
        name="regroup",
        out_shape=(
            pltpu.VMEM((128 * 48, 128), jnp.float32),
            pltpu.VMEM(grad.shape, jnp.float32),
            pltpu.VMEM((1, 128), jnp.float32),
        ),
        in_specs=[hbm] * 4,
        out_specs=(vmem, vmem, vmem),
        scratch_shapes=[
            pltpu.VMEM((3, ROWS, MATS, D), jnp.float32),
            pltpu.VMEM((128, 45, 128), jnp.float32),
            pltpu.VMEM((1, 1, 128), jnp.float32),
            pltpu.VMEM((16, 1, 128), jnp.float32),
            pltpu.VMEM((8, 1, 128), jnp.float32),
            pltpu.VMEM((1, 1, 128), jnp.float32),
            pltpu.SemaphoreType.DMA((8,)),
            pltpu.SemaphoreType.DMA,
            pltpu.SemaphoreType.DMA,
            pltpu.SemaphoreType.DMA,
            pltpu.SemaphoreType.DMA,
            pltpu.SemaphoreType.DMA,
            pltpu.SemaphoreType.DMA,
            pltpu.SemaphoreType.DMA,
            pltpu.SemaphoreType.REGULAR,
        ],
        compiler_params=pltpu.CompilerParams(
            collective_id=0, has_side_effects=True, vmem_limit_bytes=24 * 2**20
        ),
    )(*stored, grad)
    return pl.pallas_call(
        adamw,
        name="adamw",
        out_shape=(shape, shape, shape),
        in_specs=[vmem] * 3,
        out_specs=(hbm, hbm, hbm),
        scratch_shapes=[
            pltpu.VMEM((6, MATS, 128, 128), jnp.float32),
            pltpu.VMEM((3, MATS, BLOCK, 768), jnp.float32),
            pltpu.SemaphoreType.DMA,
        ],
        compiler_params=pltpu.CompilerParams(vmem_limit_bytes=24 * 2**20),
    )(arrived, gv, total)


def solution(mesh):
    placed = (
        P(None, ("dp", "tensor"), None),
        P(None, ("dp", "tensor"), None),
        P(None, ("dp", "tensor"), None),
        P(None, "dp", "tensor"),
    )
    return jax.shard_map(
        local,
        mesh=mesh,
        in_specs=placed,
        out_specs=(P(None, "dp", "tensor"), P(None, "dp", "tensor"), P(None, "dp", "tensor")),
        check_vma=False,
    )
```

```python
import jax
import jax.numpy as jnp
from jax import lax
from jax.experimental import pallas as pl
from jax.experimental.pallas import tpu as pltpu
from jax.sharding import PartitionSpec as P

D = 5120
MOE_FF = 1536
MATS = 8
ROWS = 6
BLOCK = 40
MESH = pl.DeviceIdType.MESH

bias_first = 0.9999734386011124
bias_second = 0.994079470779666
COUNT = float(MATS * D * MOE_FF)


def pack_group(xin, src, zt):
    lane = lax.broadcasted_iota(jnp.int32, (8, 128), 1)
    row = lax.broadcasted_iota(jnp.int32, (8, 128), 0)
    low = row < 3
    off1 = jnp.where(low, 80, 72)
    off2 = jnp.where(low, 120, jnp.where(row == 3, 104, 88))
    base = pl.multiple_of(zt * 640, 128)

    def load(a, h, t):
        return xin[a, h, :, pl.ds(base + 128 * t, 128)]

    for h in range(ROWS):
        tiles = [
            [load(a, h, t) if a == 0 else pltpu.roll(load(a, h, t), 40 * a, 1) for t in range(5)]
            for a in range(3)
        ]
        if h < 5:
            extra = [pltpu.roll(load(2, 5, t), 120 - 8 * h, 1) for t in range(5)]
        else:
            fill1, fill2 = [], []
            for t in range(5):
                x, y = load(0, 5, t), load(1, 5, t)
                up = [pltpu.roll(pltpu.roll(y, 8 - d, 0), k, 1) for d, k in ((5, 120), (2, 72), (4, 104), (3, 88))]
                fill1.append(jnp.where(low, pltpu.roll(pltpu.roll(x, 3, 0), 80, 1), up[1]))
                fill2.append(jnp.where(low, up[0], jnp.where(row == 3, up[2], up[3])))
        for p in range(16):
            start = (40 * p) % 128
            t0 = (40 * p) // 128
            u = (lane + (128 - start)) & 127
            split = start + 40 > 128

            def pick(v, offset):
                if not split:
                    return v[t0]
                return jnp.where(u - offset < 128 - start, v[t0], v[t0 + 1])

            first, second = pick(tiles[0], 0), pick(tiles[1], 40)
            if h < 5:
                third = pick(tiles[2], 80)
                out = jnp.where(u < 40, first, jnp.where(u < 80, second, third))
                src[zt * 16 + p, 8 * h : 8 * h + 8, :] = jnp.where(
                    u < 120, out, extra[(5 * p + h) // 16]
                )
            else:
                last = jnp.logical_or(u >= 120, jnp.logical_and(u >= 112, row >= 3))
                third = jnp.where(last, pick(fill2, off2), pick(fill1, off1))
                out = jnp.where(u < 40, first, jnp.where(u < 80, second, third))
                src[zt * 16 + p, 40:45, :] = out[0:5]


def flip(arr, wide, grp, m):
    for t in range(3):
        start = pl.multiple_of(grp * 3072, 8) + t * 1024 + m
        wide[m][t] = arr[pl.ds(start, 128, 8), :].T


def update(wide, gv, scale, grp, m, out):
    plane = lax.axis_index("dp") % 16
    lane = lax.broadcasted_iota(jnp.int32, (8, 128), 1)
    sixth = [(lane + 128 * t) % 6 == 5 for t in range(3)]
    spots = [pl.multiple_of(8 * ((5 * plane + j) % 16), 8) for j in range(16)]

    def slot(t, mat, j):
        return wide[mat][t, pl.ds(spots[j], 8), :]

    spare = [slot(t, m, 15) for t in range(3)]
    for w in range(5):
        moved = [pltpu.roll(v, 5 - w, 1) for v in spare]
        for t in range(3):
            rows = slice(8 * w, 8 * w + 8)
            cols = slice(128 * t, 128 * t + 128)
            weights = slot(t, m, w)
            first = slot(t, m, 5 + w)
            back = moved[t] if t == 0 else jnp.where(lane < 5 - w, moved[t - 1], moved[t])
            second = jnp.where(sixth[t], back, slot(t, m, 10 + w))
            if m >= 5:
                weights = jnp.where(sixth[t], slot(t, m - 5, 10 + w), weights)
                if w == 0:
                    other = slot(t, m - 5, 15)
                elif m < 7:
                    other = slot(t, m - 2, 9 + w)
                else:
                    other = slot(t, 3 + (w - 1) // 2, 14 + (w - 1) % 2)
                first = jnp.where(sixth[t], other, first)
            clipped = scale * gv[m, rows, pl.ds(pl.multiple_of(grp * 384, 128) + 128 * t, 128)]
            new_first = 0.9 * first + 0.1 * clipped
            new_second = 0.95 * second + 0.05 * clipped * clipped
            step = new_first / bias_first / (jnp.sqrt(new_second / bias_second) + 1e-08)
            out(0, rows, cols, weights * (1.0 - 0.05 * 0.1) - 0.05 * step)
            out(1, rows, cols, new_first)
            out(2, rows, cols, new_second)


def regroup(
    x0, x1, x2, g_hbm, arr, gv, scale_out, early,
    xin, src, mine_sum, plane_sums, col_sums, sib_sum, w0, w1, w2, w3, w4, w5, w6, w7,
    in_sem, g_sem, send_sem, recv_sem, small_send, plane_recv, col_recv, sib_recv, col_sem,
):
    wide = (w0, w1, w2, w3, w4, w5, w6, w7)
    s = lax.axis_index("dp")
    c = lax.axis_index("tensor")
    z = s // 16
    plane = s % 16
    half = z // 4
    dl = 2 * (s % 64) + c
    mine = half == c

    barrier = pltpu.get_barrier_semaphore()
    for i in range(1, 16):
        for core in range(2):
            pl.semaphore_signal(barrier, inc=1, device_id=(s ^ i, core), device_id_type=MESH)
    for i in range(1, 8):
        pl.semaphore_signal(barrier, inc=1, device_id=(s ^ (16 * i), c), device_id_type=MESH)
    pl.semaphore_signal(barrier, inc=1, device_id=(s, 1 - c), device_id_type=MESH)

    def in_copies(zt):
        cols = pl.ds(pl.multiple_of(zt * 640, 128), 640)
        return [
            pltpu.make_async_copy(x.at[:, :, cols], xin.at[a, :, :, cols], in_sem.at[zt])
            for a, x in enumerate((x0, x1, x2))
        ]

    for zt in range(8):
        for copy in in_copies(zt):
            copy.start()
    gcopy = pltpu.make_async_copy(g_hbm, gv, g_sem)
    gcopy.start()

    def pack(zt, carry):
        for copy in in_copies(zt):
            copy.wait()
        pack_group(xin, src, zt)
        return carry

    pl.semaphore_wait(barrier, 38)
    for i in range(1, 8):
        pl.semaphore_signal(col_sem, inc=1, device_id=(s ^ (16 * i), c), device_id_type=MESH)
    lax.fori_loop(0, 8, pack, 0)
    pl.semaphore_wait(col_sem, 7)

    slot = arr.at[pl.ds(pl.multiple_of(48 * dl, 8), 45)]

    def send(offsets, r, j, sem):
        kz = offsets[r]
        t = s ^ (16 * kz) ^ (j ^ (4 * r))
        message = pltpu.make_async_remote_copy(
            src_ref=src.at[t],
            dst_ref=slot,
            send_sem=send_sem,
            recv_sem=sem,
            device_id=(t, half),
            device_id_type=MESH,
        )
        if kz > 0:
            message.start()
        else:
            own = jnp.logical_and(j == 4 * r, mine)
            pl.when(jnp.logical_not(own))(message.start)
            pl.when(own)(pltpu.make_async_copy(src.at[t], slot, sem).start)

    def first_phase(j, carry):
        for r in range(4):
            send((7, 2, 6, 3), r, j, recv_sem.at[0])
        return carry

    lates = [4 * jnp.minimum(z ^ kz, 4) for kz in (4, 1, 5, 0)]

    def second_phase(q, carry):
        for r in range(4):
            j = q - lates[r]
            inside = jnp.logical_and(j >= 0, j < 16)
            pl.when(inside)(lambda: send((4, 1, 5, 0), r, j, recv_sem.at[1]))
        return carry

    def small(dst, recv, peer, core):
        return pltpu.make_async_remote_copy(
            src_ref=mine_sum,
            dst_ref=dst,
            send_sem=small_send,
            recv_sem=recv,
            device_id=(peer, core),
            device_id_type=MESH,
        )

    lax.fori_loop(0, 4, first_phase, 0)

    gcopy.wait()

    def squares(m, acc):
        for i in range(5):
            for j in range(6):
                v = gv[m, 8 * i : 8 * i + 8, 128 * j : 128 * j + 128]
                acc = acc + v * v
        return acc

    acc = lax.fori_loop(0, MATS, squares, jnp.zeros((8, 128), jnp.float32))
    part = jnp.broadcast_to(jnp.sum(acc, axis=(0, 1), keepdims=True), (1, 128))
    mine_sum[0] = part
    plane_sums[plane] = part
    plane_out = [small(plane_sums.at[pl.ds(plane, 1)], plane_recv, s ^ i, c) for i in range(1, 16)]
    for copy in plane_out:
        copy.start()
    lax.fori_loop(4, 16, first_phase, 0)
    for copy in plane_out:
        copy.wait_send()
    first15 = plane_sums.at[pl.ds(0, 15)]
    pltpu.make_async_copy(first15, first15, plane_recv).wait()
    part = jnp.sum(plane_sums[...], axis=0)
    mine_sum[0] = part
    col_sums[z] = part
    col_out = [small(col_sums.at[pl.ds(z, 1)], col_recv, s ^ (16 * i), c) for i in range(1, 8)]
    for copy in col_out:
        copy.start()
    lax.fori_loop(0, 32, second_phase, 0)
    for copy in col_out:
        copy.wait_send()
    first7 = col_sums.at[pl.ds(0, 7)]
    pltpu.make_async_copy(first7, first7, col_recv).wait()
    part = jnp.sum(col_sums[...], axis=0)
    mine_sum[0] = part
    swap = small(sib_sum, sib_recv, s, 1 - c)
    swap.start()
    swap.wait()
    limit = 0.5 * jnp.sqrt(jnp.float32(COUNT))
    scale = jnp.minimum(1.0, limit / (jnp.sqrt(part + sib_sum[0]) + 1e-06))
    scale = jnp.broadcast_to(scale, (8, 128))
    scale_out[...] = scale

    some = src.at[pl.ds(0, 64)]
    pltpu.make_async_copy(some, some, recv_sem.at[0]).wait()
    grp = 1 - (z // 2) % 2
    for m in range(MATS):
        flip(arr, wide, grp, m)

        def keep(a, rows, cols, value):
            early[a, m, rows, cols] = value

        update(wide, gv, scale, grp, m, keep)

    pltpu.make_async_copy(some, some, recv_sem.at[1]).wait()
    sent = src.at[pl.ds(0, 127)]
    pltpu.make_async_copy(sent, sent, send_sem).wait()

    @pl.when(jnp.logical_not(mine))
    def _():
        pltpu.make_async_copy(src.at[127], src.at[127], send_sem).wait()


def adamw(
    arr, gv, scale_in, early, o0, o1, o2,
    late, w0, w1, w2, w3, w4, w5, w6, w7, early_sem, late_sem,
):
    wide = (w0, w1, w2, w3, w4, w5, w6, w7)
    grp = (lax.axis_index("dp") // 32) % 2
    there = pl.ds(pl.multiple_of(384 * (1 - grp), 128), 384)
    here = pl.ds(pl.multiple_of(384 * grp, 128), 384)
    outs = (o0, o1, o2)
    early_out = [
        pltpu.make_async_copy(early.at[a, m], o.at[m, :, there], early_sem)
        for m in range(MATS)
        for a, o in enumerate(outs)
    ]
    for copy in early_out:
        copy.start()
    scale = scale_in[...]
    late_out = []
    flip(arr, wide, grp, 0)
    for m in range(MATS):
        if m + 1 < MATS:
            flip(arr, wide, grp, m + 1)

        def keep(a, rows, cols, value):
            late[a, m, rows, cols] = value

        update(wide, gv, scale, grp, m, keep)
        for a, o in enumerate(outs):
            late_out.append(pltpu.make_async_copy(late.at[a, m], o.at[m, :, here], late_sem))
            late_out[-1].start()
    for a in range(3):
        pltpu.make_async_copy(early.at[a], early.at[a], early_sem).wait()
        pltpu.make_async_copy(late.at[a], late.at[a], late_sem).wait()


def local(master, moment_one, moment_two, grad):
    shape = jax.ShapeDtypeStruct(grad.shape, jnp.float32)
    hbm = pl.BlockSpec(memory_space=pltpu.HBM)
    vmem = pl.BlockSpec(memory_space=pltpu.VMEM)
    stored = [
        pltpu.with_memory_space_constraint(jnp.transpose(x, (1, 0, 2)), pltpu.HBM)
        for x in (master, moment_one, moment_two)
    ]
    grad = pltpu.with_memory_space_constraint(grad, pltpu.HBM)
    wide = [pltpu.VMEM((3, 128, 128), jnp.float32)] * MATS
    half = (3, MATS, BLOCK, 384)
    arrived, gv, scale, early = pl.pallas_call(
        regroup,
        name="regroup",
        out_shape=(
            pltpu.VMEM((128 * 48, 128), jnp.float32),
            pltpu.VMEM(grad.shape, jnp.float32),
            pltpu.VMEM((8, 128), jnp.float32),
            pltpu.VMEM(half, jnp.float32),
        ),
        in_specs=[hbm] * 4,
        out_specs=(vmem, vmem, vmem, vmem),
        scratch_shapes=[
            pltpu.VMEM((3, ROWS, MATS, D), jnp.float32),
            pltpu.VMEM((128, 45, 128), jnp.float32),
            pltpu.VMEM((1, 1, 128), jnp.float32),
            pltpu.VMEM((16, 1, 128), jnp.float32),
            pltpu.VMEM((8, 1, 128), jnp.float32),
            pltpu.VMEM((1, 1, 128), jnp.float32),
            *wide,
            pltpu.SemaphoreType.DMA((8,)),
            pltpu.SemaphoreType.DMA,
            pltpu.SemaphoreType.DMA,
            pltpu.SemaphoreType.DMA((2,)),
            pltpu.SemaphoreType.DMA,
            pltpu.SemaphoreType.DMA,
            pltpu.SemaphoreType.DMA,
            pltpu.SemaphoreType.DMA,
            pltpu.SemaphoreType.REGULAR,
        ],
        compiler_params=pltpu.CompilerParams(
            collective_id=0, has_side_effects=True, vmem_limit_bytes=24 * 2**20
        ),
    )(*stored, grad)
    return pl.pallas_call(
        adamw,
        name="adamw",
        out_shape=(shape, shape, shape),
        in_specs=[vmem] * 4,
        out_specs=(hbm, hbm, hbm),
        scratch_shapes=[
            pltpu.VMEM(half, jnp.float32),
            *wide,
            pltpu.SemaphoreType.DMA,
            pltpu.SemaphoreType.DMA,
        ],
        compiler_params=pltpu.CompilerParams(vmem_limit_bytes=24 * 2**20),
    )(arrived, gv, scale, early)


def solution(mesh):
    placed = (
        P(None, ("dp", "tensor"), None),
        P(None, ("dp", "tensor"), None),
        P(None, ("dp", "tensor"), None),
        P(None, "dp", "tensor"),
    )
    return jax.shard_map(
        local,
        mesh=mesh,
        in_specs=placed,
        out_specs=(P(None, "dp", "tensor"), P(None, "dp", "tensor"), P(None, "dp", "tensor")),
        check_vma=False,
    )
```

```python
import jax
import jax.numpy as jnp
from jax import lax
from jax.experimental import pallas as pl
from jax.experimental.pallas import tpu as pltpu
from jax.sharding import PartitionSpec as P

D = 5120
MOE_FF = 1536
MATS = 8
ROWS = 6
BLOCK = 40
MESH = pl.DeviceIdType.MESH

bias_first = 0.9999734386011124
bias_second = 0.994079470779666
COUNT = float(MATS * D * MOE_FF)


FIRST = (7, 6, 2, 3)
BEGIN = {7: 0, 6: 0, 2: 8, 3: 8, 4: 16, 5: 16, 1: 24, 0: 24}
SKEW = {7: 0, 2: 1, 6: 2, 3: 3, 4: 0, 1: 1, 5: 2, 0: 3}
LATER = (2, 2)


def pack_group(xin, src, zt):
    lane = lax.broadcasted_iota(jnp.int32, (8, 128), 1)
    row = lax.broadcasted_iota(jnp.int32, (8, 128), 0)
    low = row < 3
    off1 = jnp.where(low, 80, 72)
    off2 = jnp.where(low, 120, jnp.where(row == 3, 104, 88))
    base = pl.multiple_of(zt * 640, 128)

    def load(a, h, t):
        return xin[a, h, :, pl.ds(base + 128 * t, 128)]

    for h in range(ROWS):
        tiles = [
            [load(a, h, t) if a == 0 else pltpu.roll(load(a, h, t), 40 * a, 1) for t in range(5)]
            for a in range(3)
        ]
        if h < 5:
            extra = [pltpu.roll(load(2, 5, t), 120 - 8 * h, 1) for t in range(5)]
        else:
            fill1, fill2 = [], []
            for t in range(5):
                x, y = load(0, 5, t), load(1, 5, t)
                up = [pltpu.roll(pltpu.roll(y, 8 - d, 0), k, 1) for d, k in ((5, 120), (2, 72), (4, 104), (3, 88))]
                fill1.append(jnp.where(low, pltpu.roll(pltpu.roll(x, 3, 0), 80, 1), up[1]))
                fill2.append(jnp.where(low, up[0], jnp.where(row == 3, up[2], up[3])))
        for p in range(16):
            start = (40 * p) % 128
            t0 = (40 * p) // 128
            u = (lane + (128 - start)) & 127
            split = start + 40 > 128

            def pick(v, offset):
                if not split:
                    return v[t0]
                return jnp.where(u - offset < 128 - start, v[t0], v[t0 + 1])

            first, second = pick(tiles[0], 0), pick(tiles[1], 40)
            if h < 5:
                third = pick(tiles[2], 80)
                out = jnp.where(u < 40, first, jnp.where(u < 80, second, third))
                src[zt * 16 + p, 8 * h : 8 * h + 8, :] = jnp.where(
                    u < 120, out, extra[(5 * p + h) // 16]
                )
            else:
                last = jnp.logical_or(u >= 120, jnp.logical_and(u >= 112, row >= 3))
                third = jnp.where(last, pick(fill2, off2), pick(fill1, off1))
                out = jnp.where(u < 40, first, jnp.where(u < 80, second, third))
                src[zt * 16 + p, 40:45, :] = out[0:5]


def flip(arr, wide, grp, m):
    for t in range(3):
        start = pl.multiple_of(grp * 3072, 8) + t * 1024 + m
        wide[m][t] = arr[pl.ds(start, 128, 8), :].T


def update(wide, gv, scale, grp, m, out):
    plane = lax.axis_index("dp") % 16
    lane = lax.broadcasted_iota(jnp.int32, (8, 128), 1)
    sixth = [(lane + 128 * t) % 6 == 5 for t in range(3)]
    spots = [pl.multiple_of(8 * ((5 * plane + j) % 16), 8) for j in range(16)]

    def slot(t, mat, j):
        return wide[mat][t, pl.ds(spots[j], 8), :]

    spare = [slot(t, m, 15) for t in range(3)]
    for w in range(5):
        moved = [pltpu.roll(v, 5 - w, 1) for v in spare]
        for t in range(3):
            rows = slice(8 * w, 8 * w + 8)
            cols = slice(128 * t, 128 * t + 128)
            weights = slot(t, m, w)
            first = slot(t, m, 5 + w)
            back = moved[t] if t == 0 else jnp.where(lane < 5 - w, moved[t - 1], moved[t])
            second = jnp.where(sixth[t], back, slot(t, m, 10 + w))
            if m >= 5:
                weights = jnp.where(sixth[t], slot(t, m - 5, 10 + w), weights)
                if w == 0:
                    other = slot(t, m - 5, 15)
                elif m < 7:
                    other = slot(t, m - 2, 9 + w)
                else:
                    other = slot(t, 3 + (w - 1) // 2, 14 + (w - 1) % 2)
                first = jnp.where(sixth[t], other, first)
            clipped = scale * gv[m, rows, pl.ds(pl.multiple_of(grp * 384, 128) + 128 * t, 128)]
            new_first = 0.9 * first + 0.1 * clipped
            new_second = 0.95 * second + 0.05 * clipped * clipped
            step = new_first / bias_first / (jnp.sqrt(new_second / bias_second) + 1e-08)
            out(0, rows, cols, weights * (1.0 - 0.05 * 0.1) - 0.05 * step)
            out(1, rows, cols, new_first)
            out(2, rows, cols, new_second)


def regroup(
    x0, x1, x2, g_hbm, arr, gv, scale_out, early,
    xin, src, mine_sum, plane_sums, col_sums, sib_sum, w0, w1, w2, w3, w4, w5, w6, w7,
    in_sem, g_sem, send_sem, recv_sem, small_send, plane_recv, col_recv, sib_recv, col_sem,
):
    wide = (w0, w1, w2, w3, w4, w5, w6, w7)
    s = lax.axis_index("dp")
    c = lax.axis_index("tensor")
    z = s // 16
    plane = s % 16
    half = z // 4
    dl = 2 * (s % 64) + c
    mine = half == c

    barrier = pltpu.get_barrier_semaphore()
    for i in range(1, 16):
        for core in range(2):
            pl.semaphore_signal(barrier, inc=1, device_id=(s ^ i, core), device_id_type=MESH)
    for i in range(1, 8):
        pl.semaphore_signal(barrier, inc=1, device_id=(s ^ (16 * i), c), device_id_type=MESH)
    pl.semaphore_signal(barrier, inc=1, device_id=(s, 1 - c), device_id_type=MESH)

    def in_copies(zt):
        cols = pl.ds(pl.multiple_of(zt * 640, 128), 640)
        return [
            pltpu.make_async_copy(x.at[:, :, cols], xin.at[a, :, :, cols], in_sem.at[zt])
            for a, x in enumerate((x0, x1, x2))
        ]

    for zt in range(8):
        for copy in in_copies(zt):
            copy.start()
    gcopy = pltpu.make_async_copy(g_hbm, gv, g_sem)
    gcopy.start()

    def pack(zt, carry):
        for copy in in_copies(zt):
            copy.wait()
        pack_group(xin, src, zt)
        return carry

    pl.semaphore_wait(barrier, 38)
    for i in range(1, 8):
        pl.semaphore_signal(col_sem, inc=1, device_id=(s ^ (16 * i), c), device_id_type=MESH)
    lax.fori_loop(0, 8, pack, 0)
    pl.semaphore_wait(col_sem, 7)

    slot = arr.at[pl.ds(pl.multiple_of(48 * dl, 8), 45)]

    begins = {}
    for kz, begin in BEGIN.items():
        begins[kz] = begin if kz in FIRST else begin + LATER[kz // 4] * jnp.minimum(z ^ kz, 4)

    def turn(q, carry):
        for kz, r in SKEW.items():
            j = q - begins[kz]
            t = s ^ (16 * kz) ^ (j ^ (4 * r))
            sem = recv_sem.at[0 if kz in FIRST else 1]
            message = pltpu.make_async_remote_copy(
                src_ref=src.at[t],
                dst_ref=slot,
                send_sem=send_sem,
                recv_sem=sem,
                device_id=(t, half),
                device_id_type=MESH,
            )
            inside = jnp.logical_and(j >= 0, j < 16)
            if kz > 0:
                pl.when(inside)(message.start)
            else:
                own = jnp.logical_and(j == 4 * r, mine)
                pl.when(jnp.logical_and(inside, jnp.logical_not(own)))(message.start)
                pl.when(own)(pltpu.make_async_copy(src.at[t], slot, sem).start)
        return carry

    def small(dst, recv, peer, core):
        return pltpu.make_async_remote_copy(
            src_ref=mine_sum,
            dst_ref=dst,
            send_sem=small_send,
            recv_sem=recv,
            device_id=(peer, core),
            device_id_type=MESH,
        )

    lax.fori_loop(0, 4, turn, 0)

    gcopy.wait()

    def squares(m, acc):
        for i in range(5):
            for j in range(6):
                v = gv[m, 8 * i : 8 * i + 8, 128 * j : 128 * j + 128]
                acc = acc + v * v
        return acc

    acc = lax.fori_loop(0, MATS, squares, jnp.zeros((8, 128), jnp.float32))
    part = jnp.broadcast_to(jnp.sum(acc, axis=(0, 1), keepdims=True), (1, 128))
    mine_sum[0] = part
    plane_sums[plane] = part
    plane_out = [small(plane_sums.at[pl.ds(plane, 1)], plane_recv, s ^ i, c) for i in range(1, 16)]
    for copy in plane_out:
        copy.start()
    lax.fori_loop(4, 12, turn, 0)
    for copy in plane_out:
        copy.wait_send()
    first15 = plane_sums.at[pl.ds(0, 15)]
    pltpu.make_async_copy(first15, first15, plane_recv).wait()
    part = jnp.sum(plane_sums[...], axis=0)
    mine_sum[0] = part
    col_sums[z] = part
    col_out = [small(col_sums.at[pl.ds(z, 1)], col_recv, s ^ (16 * i), c) for i in range(1, 8)]
    for copy in col_out:
        copy.start()
    lax.fori_loop(12, 48, turn, 0)
    for copy in col_out:
        copy.wait_send()
    first7 = col_sums.at[pl.ds(0, 7)]
    pltpu.make_async_copy(first7, first7, col_recv).wait()
    part = jnp.sum(col_sums[...], axis=0)
    mine_sum[0] = part
    swap = small(sib_sum, sib_recv, s, 1 - c)
    swap.start()
    swap.wait()
    limit = 0.5 * jnp.sqrt(jnp.float32(COUNT))
    scale = jnp.minimum(1.0, limit / (jnp.sqrt(part + sib_sum[0]) + 1e-06))
    scale = jnp.broadcast_to(scale, (8, 128))
    scale_out[...] = scale

    some = src.at[pl.ds(0, 64)]
    pltpu.make_async_copy(some, some, recv_sem.at[0]).wait()
    grp = 1 - (z // 2) % 2
    for m in range(MATS):
        flip(arr, wide, grp, m)

        def keep(a, rows, cols, value):
            early[a, m, rows, cols] = value

        update(wide, gv, scale, grp, m, keep)

    pltpu.make_async_copy(some, some, recv_sem.at[1]).wait()
    sent = src.at[pl.ds(0, 127)]
    pltpu.make_async_copy(sent, sent, send_sem).wait()

    @pl.when(jnp.logical_not(mine))
    def _():
        pltpu.make_async_copy(src.at[127], src.at[127], send_sem).wait()


def adamw(
    arr, gv, scale_in, early, o0, o1, o2,
    late, w0, w1, w2, w3, w4, w5, w6, w7, early_sem, late_sem,
):
    wide = (w0, w1, w2, w3, w4, w5, w6, w7)
    grp = (lax.axis_index("dp") // 32) % 2
    there = pl.ds(pl.multiple_of(384 * (1 - grp), 128), 384)
    here = pl.ds(pl.multiple_of(384 * grp, 128), 384)
    outs = (o0, o1, o2)
    early_out = [
        pltpu.make_async_copy(early.at[a, m], o.at[m, :, there], early_sem)
        for m in range(MATS)
        for a, o in enumerate(outs)
    ]
    for copy in early_out:
        copy.start()
    scale = scale_in[...]
    late_out = []
    flip(arr, wide, grp, 0)
    for m in range(MATS):
        if m + 1 < MATS:
            flip(arr, wide, grp, m + 1)

        def keep(a, rows, cols, value):
            late[a, m, rows, cols] = value

        update(wide, gv, scale, grp, m, keep)
        for a, o in enumerate(outs):
            late_out.append(pltpu.make_async_copy(late.at[a, m], o.at[m, :, here], late_sem))
            late_out[-1].start()
    for a in range(3):
        pltpu.make_async_copy(early.at[a], early.at[a], early_sem).wait()
        pltpu.make_async_copy(late.at[a], late.at[a], late_sem).wait()


def local(master, moment_one, moment_two, grad):
    shape = jax.ShapeDtypeStruct(grad.shape, jnp.float32)
    hbm = pl.BlockSpec(memory_space=pltpu.HBM)
    vmem = pl.BlockSpec(memory_space=pltpu.VMEM)
    stored = [
        pltpu.with_memory_space_constraint(jnp.transpose(x, (1, 0, 2)), pltpu.HBM)
        for x in (master, moment_one, moment_two)
    ]
    grad = pltpu.with_memory_space_constraint(grad, pltpu.HBM)
    wide = [pltpu.VMEM((3, 128, 128), jnp.float32)] * MATS
    half = (3, MATS, BLOCK, 384)
    arrived, gv, scale, early = pl.pallas_call(
        regroup,
        name="regroup",
        out_shape=(
            pltpu.VMEM((128 * 48, 128), jnp.float32),
            pltpu.VMEM(grad.shape, jnp.float32),
            pltpu.VMEM((8, 128), jnp.float32),
            pltpu.VMEM(half, jnp.float32),
        ),
        in_specs=[hbm] * 4,
        out_specs=(vmem, vmem, vmem, vmem),
        scratch_shapes=[
            pltpu.VMEM((3, ROWS, MATS, D), jnp.float32),
            pltpu.VMEM((128, 45, 128), jnp.float32),
            pltpu.VMEM((1, 1, 128), jnp.float32),
            pltpu.VMEM((16, 1, 128), jnp.float32),
            pltpu.VMEM((8, 1, 128), jnp.float32),
            pltpu.VMEM((1, 1, 128), jnp.float32),
            *wide,
            pltpu.SemaphoreType.DMA((8,)),
            pltpu.SemaphoreType.DMA,
            pltpu.SemaphoreType.DMA,
            pltpu.SemaphoreType.DMA((2,)),
            pltpu.SemaphoreType.DMA,
            pltpu.SemaphoreType.DMA,
            pltpu.SemaphoreType.DMA,
            pltpu.SemaphoreType.DMA,
            pltpu.SemaphoreType.REGULAR,
        ],
        compiler_params=pltpu.CompilerParams(
            collective_id=0, has_side_effects=True, vmem_limit_bytes=24 * 2**20
        ),
    )(*stored, grad)
    return pl.pallas_call(
        adamw,
        name="adamw",
        out_shape=(shape, shape, shape),
        in_specs=[vmem] * 4,
        out_specs=(hbm, hbm, hbm),
        scratch_shapes=[
            pltpu.VMEM(half, jnp.float32),
            *wide,
            pltpu.SemaphoreType.DMA,
            pltpu.SemaphoreType.DMA,
        ],
        compiler_params=pltpu.CompilerParams(vmem_limit_bytes=24 * 2**20),
    )(arrived, gv, scale, early)


def solution(mesh):
    placed = (
        P(None, ("dp", "tensor"), None),
        P(None, ("dp", "tensor"), None),
        P(None, ("dp", "tensor"), None),
        P(None, "dp", "tensor"),
    )
    return jax.shard_map(
        local,
        mesh=mesh,
        in_specs=placed,
        out_specs=(P(None, "dp", "tensor"), P(None, "dp", "tensor"), P(None, "dp", "tensor")),
        check_vma=False,
    )
```

```python
import jax
import jax.numpy as jnp
from jax import lax
from jax.experimental import pallas as pl
from jax.experimental.pallas import tpu as pltpu
from jax.sharding import PartitionSpec as P

D = 5120
MOE_FF = 1536
MATS = 8
ROWS = 6
BLOCK = 40
MESH = pl.DeviceIdType.MESH

bias_first = 0.9999734386011124
bias_second = 0.994079470779666
COUNT = float(MATS * D * MOE_FF)


FIRST = (7, 6, 2, 3)
BEGIN = {7: 0, 6: 0, 2: 8, 3: 8, 4: 16, 5: 16, 1: 24, 0: 24}
SKEW = {7: 0, 2: 1, 6: 2, 3: 3, 4: 0, 1: 1, 5: 2, 0: 3}
LATER = (2, 2)


def pack_group(xin, src, zt):
    lane = lax.broadcasted_iota(jnp.int32, (8, 128), 1)
    row = lax.broadcasted_iota(jnp.int32, (8, 128), 0)
    low = row < 3
    off1 = jnp.where(low, 80, 72)
    off2 = jnp.where(low, 120, jnp.where(row == 3, 104, 88))
    base = pl.multiple_of(zt * 640, 128)

    def load(a, h, t):
        return xin[a, h, :, pl.ds(base + 128 * t, 128)]

    for h in range(ROWS):
        tiles = [
            [load(a, h, t) if a == 0 else pltpu.roll(load(a, h, t), 40 * a, 1) for t in range(5)]
            for a in range(3)
        ]
        if h < 5:
            extra = [pltpu.roll(load(2, 5, t), 120 - 8 * h, 1) for t in range(5)]
        else:
            fill1, fill2 = [], []
            for t in range(5):
                x, y = load(0, 5, t), load(1, 5, t)
                up = [pltpu.roll(pltpu.roll(y, 8 - d, 0), k, 1) for d, k in ((5, 120), (2, 72), (4, 104), (3, 88))]
                fill1.append(jnp.where(low, pltpu.roll(pltpu.roll(x, 3, 0), 80, 1), up[1]))
                fill2.append(jnp.where(low, up[0], jnp.where(row == 3, up[2], up[3])))
        for p in range(16):
            start = (40 * p) % 128
            t0 = (40 * p) // 128
            u = (lane + (128 - start)) & 127
            split = start + 40 > 128

            def pick(v, offset):
                if not split:
                    return v[t0]
                return jnp.where(u - offset < 128 - start, v[t0], v[t0 + 1])

            first, second = pick(tiles[0], 0), pick(tiles[1], 40)
            if h < 5:
                third = pick(tiles[2], 80)
                out = jnp.where(u < 40, first, jnp.where(u < 80, second, third))
                src[zt * 16 + p, 8 * h : 8 * h + 8, :] = jnp.where(
                    u < 120, out, extra[(5 * p + h) // 16]
                )
            else:
                last = jnp.logical_or(u >= 120, jnp.logical_and(u >= 112, row >= 3))
                third = jnp.where(last, pick(fill2, off2), pick(fill1, off1))
                out = jnp.where(u < 40, first, jnp.where(u < 80, second, third))
                src[zt * 16 + p, 40:45, :] = out[0:5]


def flip(arr, wide, grp, m):
    for t in range(3):
        start = pl.multiple_of(grp * 3072, 8) + t * 1024 + m
        wide[m][t] = arr[pl.ds(start, 128, 8), :].T


def update(wide, gv, scale, grp, m, out):
    plane = lax.axis_index("dp") % 16
    lane = lax.broadcasted_iota(jnp.int32, (8, 128), 1)
    sixth = [(lane + 128 * t) % 6 == 5 for t in range(3)]
    spots = [pl.multiple_of(8 * ((5 * plane + j) % 16), 8) for j in range(16)]

    def slot(t, mat, j):
        return wide[mat][t, pl.ds(spots[j], 8), :]

    spare = [slot(t, m, 15) for t in range(3)]
    for w in range(5):
        moved = [pltpu.roll(v, 5 - w, 1) for v in spare]
        for t in range(3):
            rows = slice(8 * w, 8 * w + 8)
            cols = slice(128 * t, 128 * t + 128)
            weights = slot(t, m, w)
            first = slot(t, m, 5 + w)
            back = moved[t] if t == 0 else jnp.where(lane < 5 - w, moved[t - 1], moved[t])
            second = jnp.where(sixth[t], back, slot(t, m, 10 + w))
            if m >= 5:
                weights = jnp.where(sixth[t], slot(t, m - 5, 10 + w), weights)
                if w == 0:
                    other = slot(t, m - 5, 15)
                elif m < 7:
                    other = slot(t, m - 2, 9 + w)
                else:
                    other = slot(t, 3 + (w - 1) // 2, 14 + (w - 1) % 2)
                first = jnp.where(sixth[t], other, first)
            clipped = scale * gv[m, rows, pl.ds(pl.multiple_of(grp * 384, 128) + 128 * t, 128)]
            new_first = 0.9 * first + 0.1 * clipped
            new_second = 0.95 * second + 0.05 * clipped * clipped
            step = new_first / bias_first / (jnp.sqrt(new_second / bias_second) + 1e-08)
            out(0, rows, cols, weights * (1.0 - 0.05 * 0.1) - 0.05 * step)
            out(1, rows, cols, new_first)
            out(2, rows, cols, new_second)


def regroup(
    x0, x1, x2, g_hbm, arr, gv, scale_out, early,
    xin, src, mine_sum, plane_sums, col_sums, sib_sum, w0, w1, w2, w3, w4, w5, w6, w7,
    in_sem, g_sem, send_sem, recv_sem, small_send, plane_recv, col_recv, sib_recv, col_sem,
):
    wide = (w0, w1, w2, w3, w4, w5, w6, w7)
    s = lax.axis_index("dp")
    c = lax.axis_index("tensor")
    z = s // 16
    plane = s % 16
    half = z // 4
    dl = 2 * (s % 64) + c
    mine = half == c

    barrier = pltpu.get_barrier_semaphore()
    for i in range(1, 16):
        for core in range(2):
            pl.semaphore_signal(barrier, inc=1, device_id=(s ^ i, core), device_id_type=MESH)
    for i in range(1, 8):
        pl.semaphore_signal(barrier, inc=1, device_id=(s ^ (16 * i), c), device_id_type=MESH)
    pl.semaphore_signal(barrier, inc=1, device_id=(s, 1 - c), device_id_type=MESH)

    def in_copies(zt):
        cols = pl.ds(pl.multiple_of(zt * 640, 128), 640)
        return [
            pltpu.make_async_copy(x.at[:, :, cols], xin.at[a, :, :, cols], in_sem.at[zt])
            for a, x in enumerate((x0, x1, x2))
        ]

    for zt in range(8):
        for copy in in_copies(zt):
            copy.start()
    gcopy = pltpu.make_async_copy(g_hbm, gv, g_sem)
    gcopy.start()

    def pack(zt, carry):
        for copy in in_copies(zt):
            copy.wait()
        pack_group(xin, src, zt)
        return carry

    pl.semaphore_wait(barrier, 38)
    for i in range(1, 8):
        pl.semaphore_signal(col_sem, inc=1, device_id=(s ^ (16 * i), c), device_id_type=MESH)
    lax.fori_loop(0, 8, pack, 0)
    pl.semaphore_wait(col_sem, 7)

    slot = arr.at[pl.ds(pl.multiple_of(48 * dl, 8), 45)]

    begins = {}
    for kz, begin in BEGIN.items():
        begins[kz] = begin if kz in FIRST else begin + LATER[kz // 4] * jnp.minimum(z ^ kz, 4)

    def turn(q, carry):
        for kz, r in SKEW.items():
            j = q - begins[kz]
            t = s ^ (16 * kz) ^ (j ^ (4 * r))
            sem = recv_sem.at[0 if kz in FIRST else 1]
            message = pltpu.make_async_remote_copy(
                src_ref=src.at[t],
                dst_ref=slot,
                send_sem=send_sem,
                recv_sem=sem,
                device_id=(t, half),
                device_id_type=MESH,
            )
            inside = jnp.logical_and(j >= 0, j < 16)
            if kz > 0:
                pl.when(inside)(message.start)
            else:
                own = jnp.logical_and(j == 4 * r, mine)
                pl.when(jnp.logical_and(inside, jnp.logical_not(own)))(message.start)
                pl.when(own)(pltpu.make_async_copy(src.at[t], slot, sem).start)
        return carry

    def small(dst, recv, peer, core):
        return pltpu.make_async_remote_copy(
            src_ref=mine_sum,
            dst_ref=dst,
            send_sem=small_send,
            recv_sem=recv,
            device_id=(peer, core),
            device_id_type=MESH,
        )

    lax.fori_loop(0, 8, turn, 0)

    gcopy.wait()

    def squares(m, acc):
        for i in range(5):
            for j in range(6):
                v = gv[m, 8 * i : 8 * i + 8, 128 * j : 128 * j + 128]
                acc = acc + v * v
        return acc

    acc = lax.fori_loop(0, MATS, squares, jnp.zeros((8, 128), jnp.float32))
    part = jnp.broadcast_to(jnp.sum(acc, axis=(0, 1), keepdims=True), (1, 128))
    mine_sum[0] = part
    plane_sums[plane] = part
    plane_out = [small(plane_sums.at[pl.ds(plane, 1)], plane_recv, s ^ i, c) for i in range(1, 16)]
    for copy in plane_out:
        copy.start()
    lax.fori_loop(8, 20, turn, 0)
    for copy in plane_out:
        copy.wait_send()
    first15 = plane_sums.at[pl.ds(0, 15)]
    pltpu.make_async_copy(first15, first15, plane_recv).wait()
    part = jnp.sum(plane_sums[...], axis=0)
    mine_sum[0] = part
    col_sums[z] = part
    col_out = [small(col_sums.at[pl.ds(z, 1)], col_recv, s ^ (16 * i), c) for i in range(1, 8)]
    for copy in col_out:
        copy.start()
    lax.fori_loop(20, 48, turn, 0)
    for copy in col_out:
        copy.wait_send()
    first7 = col_sums.at[pl.ds(0, 7)]
    pltpu.make_async_copy(first7, first7, col_recv).wait()
    part = jnp.sum(col_sums[...], axis=0)
    mine_sum[0] = part
    swap = small(sib_sum, sib_recv, s, 1 - c)
    swap.start()
    swap.wait()
    limit = 0.5 * jnp.sqrt(jnp.float32(COUNT))
    scale = jnp.minimum(1.0, limit / (jnp.sqrt(part + sib_sum[0]) + 1e-06))
    scale = jnp.broadcast_to(scale, (8, 128))
    scale_out[...] = scale

    some = src.at[pl.ds(0, 64)]
    pltpu.make_async_copy(some, some, recv_sem.at[0]).wait()
    grp = 1 - (z // 2) % 2
    for m in range(MATS):
        flip(arr, wide, grp, m)

        def keep(a, rows, cols, value):
            early[a, m, rows, cols] = value

        update(wide, gv, scale, grp, m, keep)

    pltpu.make_async_copy(some, some, recv_sem.at[1]).wait()
    sent = src.at[pl.ds(0, 127)]
    pltpu.make_async_copy(sent, sent, send_sem).wait()

    @pl.when(jnp.logical_not(mine))
    def _():
        pltpu.make_async_copy(src.at[127], src.at[127], send_sem).wait()


def adamw(
    arr, gv, scale_in, early, o0, o1, o2,
    late, w0, w1, w2, w3, w4, w5, w6, w7, early_sem, late_sem,
):
    wide = (w0, w1, w2, w3, w4, w5, w6, w7)
    grp = (lax.axis_index("dp") // 32) % 2
    there = pl.ds(pl.multiple_of(384 * (1 - grp), 128), 384)
    here = pl.ds(pl.multiple_of(384 * grp, 128), 384)
    outs = (o0, o1, o2)
    early_out = [
        pltpu.make_async_copy(early.at[a, m], o.at[m, :, there], early_sem)
        for m in range(MATS)
        for a, o in enumerate(outs)
    ]
    for copy in early_out:
        copy.start()
    scale = scale_in[...]
    late_out = []
    flip(arr, wide, grp, 0)
    for m in range(MATS):
        if m + 1 < MATS:
            flip(arr, wide, grp, m + 1)

        def keep(a, rows, cols, value):
            late[a, m, rows, cols] = value

        update(wide, gv, scale, grp, m, keep)
        for a, o in enumerate(outs):
            late_out.append(pltpu.make_async_copy(late.at[a, m], o.at[m, :, here], late_sem))
            late_out[-1].start()
    for a in range(3):
        pltpu.make_async_copy(early.at[a], early.at[a], early_sem).wait()
        pltpu.make_async_copy(late.at[a], late.at[a], late_sem).wait()


def local(master, moment_one, moment_two, grad):
    shape = jax.ShapeDtypeStruct(grad.shape, jnp.float32)
    hbm = pl.BlockSpec(memory_space=pltpu.HBM)
    vmem = pl.BlockSpec(memory_space=pltpu.VMEM)
    stored = [
        pltpu.with_memory_space_constraint(jnp.transpose(x, (1, 0, 2)), pltpu.HBM)
        for x in (master, moment_one, moment_two)
    ]
    grad = pltpu.with_memory_space_constraint(grad, pltpu.HBM)
    wide = [pltpu.VMEM((3, 128, 128), jnp.float32)] * MATS
    half = (3, MATS, BLOCK, 384)
    arrived, gv, scale, early = pl.pallas_call(
        regroup,
        name="regroup",
        out_shape=(
            pltpu.VMEM((128 * 48, 128), jnp.float32),
            pltpu.VMEM(grad.shape, jnp.float32),
            pltpu.VMEM((8, 128), jnp.float32),
            pltpu.VMEM(half, jnp.float32),
        ),
        in_specs=[hbm] * 4,
        out_specs=(vmem, vmem, vmem, vmem),
        scratch_shapes=[
            pltpu.VMEM((3, ROWS, MATS, D), jnp.float32),
            pltpu.VMEM((128, 45, 128), jnp.float32),
            pltpu.VMEM((1, 1, 128), jnp.float32),
            pltpu.VMEM((16, 1, 128), jnp.float32),
            pltpu.VMEM((8, 1, 128), jnp.float32),
            pltpu.VMEM((1, 1, 128), jnp.float32),
            *wide,
            pltpu.SemaphoreType.DMA((8,)),
            pltpu.SemaphoreType.DMA,
            pltpu.SemaphoreType.DMA,
            pltpu.SemaphoreType.DMA((2,)),
            pltpu.SemaphoreType.DMA,
            pltpu.SemaphoreType.DMA,
            pltpu.SemaphoreType.DMA,
            pltpu.SemaphoreType.DMA,
            pltpu.SemaphoreType.REGULAR,
        ],
        compiler_params=pltpu.CompilerParams(
            collective_id=0, has_side_effects=True, vmem_limit_bytes=24 * 2**20
        ),
    )(*stored, grad)
    return pl.pallas_call(
        adamw,
        name="adamw",
        out_shape=(shape, shape, shape),
        in_specs=[vmem] * 4,
        out_specs=(hbm, hbm, hbm),
        scratch_shapes=[
            pltpu.VMEM(half, jnp.float32),
            *wide,
            pltpu.SemaphoreType.DMA,
            pltpu.SemaphoreType.DMA,
        ],
        compiler_params=pltpu.CompilerParams(vmem_limit_bytes=24 * 2**20),
    )(arrived, gv, scale, early)


def solution(mesh):
    placed = (
        P(None, ("dp", "tensor"), None),
        P(None, ("dp", "tensor"), None),
        P(None, ("dp", "tensor"), None),
        P(None, "dp", "tensor"),
    )
    return jax.shard_map(
        local,
        mesh=mesh,
        in_specs=placed,
        out_specs=(P(None, "dp", "tensor"), P(None, "dp", "tensor"), P(None, "dp", "tensor")),
        check_vma=False,
    )
```
